32 devices in a mesh: ex: 4 (over y, x), tp: 4 (over z), ps: 2 (over core).
Axes of the slice: x: 2, y: 2, z: 4, core: 2. Of those that a mesh axis runs over, the one named last changes fastest.
Arguments:
- tokens: bfloat16 [1024, 8192], P(('ex', 'ps'), 'tp'), may hold values from -6 to 6
- output_gradient: bfloat16 [1024, 29568], P(('ex', 'ps'), 'tp'), may hold values from -6 to 6
- adapter_down_factor: bfloat16 [8192, 128], P('tp'), may hold values from -0.0625 to 0.0625
- adapter_up_factor: bfloat16 [29568, 128], P('tp'), may hold values from -0.03125 to 0.03125
- first_moment_down: float32 [4, 2048, 128], P('tp', ('ex', 'ps')), may hold values from -0.012 to 0.012
- second_moment_down: float32 [4, 2048, 128], P('tp', ('ex', 'ps')), may hold values from 2e-07 to 2e-06
- first_moment_up: float32 [4, 7392, 128], P('tp', ('ex', 'ps')), may hold values from -0.012 to 0.012
- second_moment_up: float32 [4, 7392, 128], P('tp', ('ex', 'ps')), may hold values from 2e-07 to 2e-06
- down_row_seeds: int32 [4, 2048], P('tp', ('ex', 'ps')), may hold values from 0 to 15
- up_row_seeds: int32 [4, 7392], P('tp', ('ex', 'ps')), may hold values from 0 to 15
- segments: int32 [1024], replicated, may hold values from 0 to 3, never falling along the last dimension, each value on 1 to 512 neighbouring positions
- bank: bfloat16 [16, 128, 8192], P(None, None, ('ex', 'tp', 'ps')), may hold values from -6 to 6
Outputs:
- sketch: float32 [4, 8192], P(None, ('ex', 'tp', 'ps'))
The draws below stay inside these ranges and needn't reach their ends.
Inputs may be any that keep to these rules, and one draw needn't show every extreme that they name: `segments`: never falls along the rows; every example has 1 to 512 rows and one has exactly 512.
All inputs are finite; a program needn't handle non-finite values.
Results may differ from the reference program's by a relative error of at most 0.0033.
Values may be sent and summed in bfloat16 or wider, within the bound.
A program may use at most 64 MiB of HBM per device.

```python
import math
import jax
import jax.numpy as jnp
import numpy as np
from jax import lax

MODEL_WIDTH = 8192
HIDDEN_WIDTH = 29568
ADAPTER_RANK = 128
K = 8192
BANK = 16
EXAMPLES = 4
TOKENS = 1024
MOST = 512
N_TP = 4


def place_ends(drawn, own_key, smallest, high):
    spot = [jax.random.randint(jax.random.fold_in(own_key, axis), (), 0, length) for axis, length in enumerate(drawn.shape)]
    widest = drawn.shape.index(max(drawn.shape))
    beside = spot[:widest] + [(spot[widest] + 1) % drawn.shape[widest]] + spot[widest + 1:]
    return drawn.at[tuple(spot)].set(smallest).at[tuple(beside)].set(high)


def steps_of(key, dims, pieces, smallest, top_value):
    factor_of = 1.0
    for axis_at, shards_of in pieces:
        heights = jax.random.uniform(jax.random.fold_in(jax.random.fold_in(key, 6), axis_at), (shards_of,), jnp.float32, smallest / len(pieces), top_value / len(pieces))
        factor_of = factor_of * jnp.repeat(jnp.exp(heights), dims[axis_at] // shards_of).reshape((-1,) + (1,) * (len(dims) - 1 - axis_at))
    return factor_of


def profile(count, total, most, lean):
    weights = [(1 << 20) // math.isqrt(standing ** lean) + 1 for standing in range(2, count + 1)]
    surplus, given = total - most - (count - 1), [1] * (count - 1)
    while surplus > 0:
        movable = [i for i in range(count - 1) if given[i] < most]
        pool, left = sum([weights[i] for i in movable]), surplus
        for i in movable:
            extra = min(most - given[i], max(1, left * weights[i] // pool), surplus)
            given[i] = given[i] + extra
            surplus = surplus - extra
    return np.array([most] + given)


def uneven_parts(stream_key, amount, total, bound, skew):
    if amount == 2:
        one = jax.random.randint(stream_key, (), max(1, total - bound), min(bound, total - 1) + 1)
        return jnp.stack([one, total - one])
    sizes = jnp.asarray(profile(amount, total, bound, skew), jnp.int32)
    couples = (amount - 1) // 2
    giver, receiver = sizes[1:1 + 2 * couples:2], sizes[2:2 + 2 * couples:2]
    margin = jnp.minimum(giver - 1, bound - receiver)
    passed = jax.random.randint(jax.random.fold_in(stream_key, 1), (couples,), 0, 1 << 20) % (margin + 1)
    sizes = sizes.at[1:1 + 2 * couples:2].set(giver - passed).at[2:2 + 2 * couples:2].set(receiver + passed)
    return sizes[jax.random.permutation(jax.random.fold_in(stream_key, 2), amount)]


def gaussian(own_key, dims, scale, reach, pieces=(), held_as=jnp.bfloat16):
    values = scale * jax.random.normal(own_key, dims, jnp.float32)
    if pieces:
        values = values * steps_of(own_key, dims, pieces, -0.22, 0.18)
    return jnp.clip(values, -reach, reach).astype(held_as)


def setup_inputs(seed: int = 0) -> dict:
    keys = jax.random.split(jax.random.key(seed), 13)
    return {
        "tokens": gaussian(keys[0], (TOKENS, MODEL_WIDTH), 1.0, 6.0, ((0, 8), (1, 4))),
        "output_gradient": gaussian(keys[1], (TOKENS, HIDDEN_WIDTH), 1.0, 6.0, ((0, 8), (1, 4))),
        "adapter_down_factor": gaussian(keys[2], (MODEL_WIDTH, ADAPTER_RANK), MODEL_WIDTH ** -0.5, 0.0625, ((0, 4),)),
        "adapter_up_factor": gaussian(keys[3], (HIDDEN_WIDTH, ADAPTER_RANK), HIDDEN_WIDTH ** -0.5, 0.03125, ((0, 4),)),
        "first_moment_down": gaussian(keys[4], (N_TP, MODEL_WIDTH // N_TP, ADAPTER_RANK), 0.002, 0.012, ((0, 4), (1, 8)), jnp.float32),
        "second_moment_down": jnp.clip(jnp.exp(math.log(1.9999999949504854e-06) - 2.3025851 * jax.random.uniform(keys[5], (N_TP, MODEL_WIDTH // N_TP, ADAPTER_RANK), jnp.float32) ** steps_of(keys[5], (N_TP, MODEL_WIDTH // N_TP, ADAPTER_RANK), ((0, 4), (1, 8)), -0.2, 0.2)), 2.0000000233721948e-07, 1.9999999949504854e-06),
        "first_moment_up": gaussian(keys[6], (N_TP, HIDDEN_WIDTH // N_TP, ADAPTER_RANK), 0.002, 0.012, ((0, 4), (1, 8)), jnp.float32),
        "second_moment_up": jnp.clip(jnp.exp(math.log(1.9999999949504854e-06) - 2.3025851 * jax.random.uniform(keys[7], (N_TP, HIDDEN_WIDTH // N_TP, ADAPTER_RANK), jnp.float32) ** steps_of(keys[7], (N_TP, HIDDEN_WIDTH // N_TP, ADAPTER_RANK), ((0, 4), (1, 8)), -0.2, 0.2)), 2.0000000233721948e-07, 1.9999999949504854e-06),
        "down_row_seeds": place_ends(jax.random.randint(keys[8], (N_TP, MODEL_WIDTH // N_TP), 0, BANK), jax.random.fold_in(keys[8], 1), 0, BANK - 1).astype(jnp.int32),
        "up_row_seeds": place_ends(jax.random.randint(keys[9], (N_TP, HIDDEN_WIDTH // N_TP), 0, BANK), jax.random.fold_in(keys[9], 1), 0, BANK - 1).astype(jnp.int32),
        "segments": jnp.searchsorted(jnp.cumsum(uneven_parts(keys[10], EXAMPLES, TOKENS, MOST, 2)), jnp.arange(TOKENS), side="right").astype(jnp.int32),
        "bank": gaussian(keys[11], (BANK, ADAPTER_RANK, K), 1.0, 6.0, ((2, 32),)),
    }


def adam_feature(grad, first, second):
    moved = 0.9 * first[None, :, :] + 0.1 * grad
    scaled = 0.999 * second[None, :, :] + 0.001 * grad * grad
    return moved / (jnp.sqrt(scaled) + 1e-08)

def reference(tokens, output_gradient, adapter_down_factor, adapter_up_factor, first_moment_down, second_moment_down, first_moment_up, second_moment_up, down_row_seeds, up_row_seeds, segments, bank):
    hidden_inner_product = jnp.dot(tokens, adapter_down_factor, preferred_element_type=jnp.float32).astype(jnp.bfloat16)
    input_inner_product = jnp.dot(output_gradient, adapter_up_factor, preferred_element_type=jnp.float32).astype(jnp.bfloat16)
    labels = jnp.arange(EXAMPLES, dtype=jnp.int32)
    counts = lax.optimization_barrier(jnp.sum((segments[None, :] == labels[:, None]).astype(jnp.int32), axis=1)).astype(jnp.int32)
    starts = (jnp.cumsum(counts) - counts).astype(jnp.int32)

    def one_example(index):
        first_row = starts[index]
        length = counts[index]
        base = jnp.minimum(first_row, TOKENS - MOST).astype(jnp.int32)
        position = base + jnp.arange(MOST, dtype=jnp.int32)
        keep = ((position >= first_row) & (position < first_row + length)).astype(tokens.dtype)[:, None]
        rows_x = lax.dynamic_slice_in_dim(tokens, base, MOST, 0)
        rows_g = lax.dynamic_slice_in_dim(output_gradient, base, MOST, 0)
        rows_u = lax.dynamic_slice_in_dim(input_inner_product, base, MOST, 0) * keep
        rows_h = lax.dynamic_slice_in_dim(hidden_inner_product, base, MOST, 0) * keep
        part_a = jnp.dot(rows_x.T, rows_u, preferred_element_type=jnp.float32)
        part_b = jnp.dot(rows_g.T, rows_h, preferred_element_type=jnp.float32)
        scale = length.astype(jnp.float32)
        return (part_a / scale, part_b / scale)
    grad_a, grad_b = lax.map(one_example, labels)
    feature_a = adam_feature(grad_a, first_moment_down.reshape(MODEL_WIDTH, ADAPTER_RANK), second_moment_down.reshape(MODEL_WIDTH, ADAPTER_RANK))
    feature_b = adam_feature(grad_b, first_moment_up.reshape(HIDDEN_WIDTH, ADAPTER_RANK), second_moment_up.reshape(HIDDEN_WIDTH, ADAPTER_RANK))
    blocks = jnp.arange(BANK, dtype=jnp.int32)
    select_a = (down_row_seeds.reshape(MODEL_WIDTH)[:, None] == blocks[None, :]).astype(jnp.float32)
    select_b = (up_row_seeds.reshape(HIDDEN_WIDTH)[:, None] == blocks[None, :]).astype(jnp.float32)
    summed = jnp.einsum('nj,enr->ejr', select_a, feature_a, precision=lax.Precision.HIGHEST)
    summed = summed + jnp.einsum('nj,enr->ejr', select_b, feature_b, precision=lax.Precision.HIGHEST)
    inverse = 1.0 / math.sqrt((MODEL_WIDTH + HIDDEN_WIDTH) * ADAPTER_RANK)
    sketch = jnp.einsum('ejr,jrk->ek', summed, bank.astype(jnp.float32), precision=lax.Precision.HIGHEST)
    return sketch * inverse
```

```python
import functools
import math

import jax
import jax.numpy as jnp
from jax import lax
from jax.experimental import pallas as pl
from jax.experimental.pallas import tpu as pltpu
from jax.sharding import PartitionSpec as P

EXAMPLES = 4
BANK = 16
MESH = pl.DeviceIdType.MESH
F32 = jnp.float32
BF16 = jnp.bfloat16


def flip(index, mask):
    out, bit = index, 1
    while bit <= mask:
        if mask & bit:
            out = out + bit - 2 * bit * ((index // bit) % 2)
        bit *= 2
    return out


def up_to(value, step):
    return -(-value // step) * step


def contract_rows(left, right):
    return lax.dot_general(left, right, (((0,), (0,)), ((), ())), preferred_element_type=F32)


def split(value, parts):
    out = []
    for _ in range(parts):
        piece = value.astype(BF16)
        out.append(piece)
        value = value - piece.astype(F32)
    return out


def kernel(
    n_ps, n_plane, n_tp, inverse,
    x_hbm, g_hbm, down_hbm, up_hbm, m1a_hbm, m2a_hbm, m1b_hbm, m2b_hbm, seeds_a, seeds_b, segments, bank_hbm,
    out_ref,
    x, g, down, up, m1a, m2a, m1b, m2b, bank,
    stage, recv, part, part_in, rank_sum, ranks, segcol, acc,
    sums, sums_in, mine, mine_in, total_in, total,
    load_sem, a2a_send, a2a_recv, rs_send, rs_recv, ag_send, ag_recv, pl_send, pl_recv,
    s1_send, s1_recv, s2_send, s2_recv, s3_send, s3_recv,
):
    ex, tp, ps = lax.axis_index("ex"), lax.axis_index("tp"), lax.axis_index("ps")
    q = ex * n_ps + ps
    chip, core = q // 2, q % 2
    n_chip = n_plane // 2
    rows = x.shape[0]
    ra, rb = m1a.shape[1], m1b.shape[1]
    pa = up_to(ra, 128)

    pairs = [(x_hbm, x), (g_hbm, g), (down_hbm, down), (up_hbm, up), (m1a_hbm, m1a), (m2a_hbm, m2a),
             (m1b_hbm, m1b), (m2b_hbm, m2b), (bank_hbm, bank)]
    loads = [pltpu.make_async_copy(a, b, load_sem.at[i]) for i, (a, b) in enumerate(pairs)]
    for load in loads:
        load.start()

    def plane_id(peer):
        return {"ex": peer // n_ps, "ps": peer % n_ps}

    def tp_id(d):
        return {"tp": (tp + d) % n_tp}

    peers = [(mask, other) for mask in range(n_chip) for other in range(2) if mask or other]

    def peer_of(mask, other):
        return 2 * flip(chip, mask) + (core + other) % 2

    barrier = pltpu.get_barrier_semaphore()
    for mask, other in peers:
        pl.semaphore_signal(barrier, inc=1, device_id=plane_id(peer_of(mask, other)), device_id_type=MESH)
    for d in range(1, n_tp):
        pl.semaphore_signal(barrier, inc=1, device_id=tp_id(d), device_id_type=MESH)

    loads[0].wait()
    loads[1].wait()
    for j in range(n_plane):
        stage[j, :, 0:ra] = x[:, j * ra:(j + 1) * ra]
        stage[j, :, pa:pa + rb] = g[:, j * rb:(j + 1) * rb]
    pl.semaphore_wait(barrier, n_plane - 1 + n_tp - 1)

    def plane_copies(src, dst, send, recv_sem, chosen):
        return [
            pltpu.make_async_remote_copy(
                src_ref=src(peer_of(mask, other)), dst_ref=dst, send_sem=send.at[mask, other],
                recv_sem=recv_sem.at[mask, other], device_id=plane_id(peer_of(mask, other)), device_id_type=MESH,
            )
            for mask, other in chosen
        ]

    a2a = plane_copies(lambda peer: stage.at[peer], recv.at[q], a2a_send, a2a_recv, peers)
    late = 2 * max(1, n_chip // 4)
    for copy in a2a[:-late]:
        copy.start()
    recv[q] = stage[q]

    loads[2].wait()
    loads[3].wait()
    part[:, 0:128] = jnp.dot(x[...], down[...], preferred_element_type=F32)
    part[:, 128:256] = jnp.dot(g[...], up[...], preferred_element_type=F32)
    slab = rows // n_tp

    def slab_at(t):
        return pl.ds(pl.multiple_of(t * slab, slab), slab)

    rs = [
        pltpu.make_async_remote_copy(
            src_ref=part.at[slab_at((tp + d) % n_tp)], dst_ref=part_in.at[d - 1], send_sem=rs_send.at[d - 1],
            recv_sem=rs_recv.at[d - 1], device_id=tp_id(d), device_id_type=MESH,
        )
        for d in range(1, n_tp)
    ]
    for copy in rs:
        copy.start()

    seg = segments[...]
    inv_len = [1.0 / jnp.sum((seg == e).astype(F32), axis=(0, 1), keepdims=True) for e in range(EXAMPLES)]
    seg_t = jnp.transpose(seg.astype(F32))
    for j in range(n_plane):
        segcol[j] = jnp.broadcast_to(seg_t[:, j:j + 1], (rows, 128))

    for copy in rs:
        copy.wait()
    summed = part[slab_at(tp), :]
    for d in range(1, n_tp):
        summed = summed + part_in[d - 1]
    rank_sum[...] = summed.astype(BF16)
    ranks[q, slab_at(tp), :] = rank_sum[...]
    ag = [
        pltpu.make_async_remote_copy(
            src_ref=rank_sum, dst_ref=ranks.at[q, slab_at(tp)], send_sem=ag_send.at[d - 1],
            recv_sem=ag_recv.at[d - 1], device_id=tp_id(d), device_id_type=MESH,
        )
        for d in range(1, n_tp)
    ]
    for copy in ag:
        copy.start()
    for copy in ag:
        copy.wait()
    gather = plane_copies(lambda peer: ranks.at[q], ranks.at[q], pl_send, pl_recv, peers)
    for copy in gather:
        copy.start()
    for copy in a2a[-late:]:
        copy.start()

    step = 256
    width = stage.shape[2]
    for mask in range(n_chip):
        for i, (m, _) in enumerate(peers):
            if m == mask:
                gather[i].wait()
                a2a[i].wait()
        first = 2 * flip(chip, mask)
        both = ranks[pl.ds(first, 2)].reshape(2 * rows, 256).astype(F32)
        labels = segcol[pl.ds(first, 2)].reshape(2 * rows, 128)
        picked_h = jnp.concatenate([jnp.where(labels == e, both[:, 0:128], 0.0) for e in range(EXAMPLES)], 1).astype(BF16)
        picked_u = jnp.concatenate([jnp.where(labels == e, both[:, 128:256], 0.0) for e in range(EXAMPLES)], 1).astype(BF16)
        spans = [(s, min(s + step, pa), picked_u) for s in range(0, pa, step)]
        spans += [(s, min(s + step, width), picked_h) for s in range(pa, width, step)]
        for lo, hi, picked in spans:
            block = recv[pl.ds(first, 2), :, lo:hi].reshape(2 * rows, hi - lo)
            term = contract_rows(block, picked)
            if mask == 0:
                acc[lo:hi, :] = term
            else:
                acc[lo:hi, :] += term

    for load in loads[4:]:
        load.wait()
    bins = lax.broadcasted_iota(jnp.int32, (BANK, 128), 0)
    summed = [jnp.zeros((BANK, 128), F32) for _ in range(EXAMPLES)]
    for base, count, m1, m2, seeds in ((0, ra, m1a, m2a, seeds_a), (pa, rb, m1b, m2b, seeds_b)):
        for lo in range(0, count, 128):
            size = min(128, count - lo)
            first = 0.9 * m1[0, lo:lo + size, :]
            second = 0.999 * m2[0, lo:lo + size, :]
            select = (seeds[:, lo:lo + size] == bins[:, :size]).astype(BF16)
            for e in range(EXAMPLES):
                grad = acc[base + lo:base + lo + size, e * 128:(e + 1) * 128] * inv_len[e]
                moved = first + 0.1 * grad
                scaled = second + 0.001 * grad * grad
                feature = moved / (jnp.sqrt(scaled) + 1e-08)
                for piece in split(feature, 2):
                    summed[e] = summed[e] + jnp.dot(select, piece, preferred_element_type=F32)

    share = sums.shape[1]
    every = jnp.concatenate(summed, axis=0)
    for j in range(n_plane):
        sums[j] = every[j * share:(j + 1) * share, :]
    scatter = plane_copies(lambda peer: sums.at[peer], sums_in.at[q], s1_send, s1_recv, peers)
    for copy in scatter:
        copy.start()
    sums_in[q] = sums[q]
    for copy in scatter:
        copy.wait()
    mine[...] = jnp.sum(sums_in[...], axis=0)
    cross = [
        pltpu.make_async_remote_copy(
            src_ref=mine, dst_ref=mine_in.at[tp], send_sem=s2_send.at[d - 1], recv_sem=s2_recv.at[d - 1],
            device_id=tp_id(d), device_id_type=MESH,
        )
        for d in range(1, n_tp)
    ]
    for copy in cross:
        copy.start()
    mine_in[tp] = mine[...]
    for copy in cross:
        copy.wait()
    total_in[q] = jnp.sum(mine_in[...], axis=0)
    spread = plane_copies(lambda peer: total_in.at[q], total_in.at[q], s3_send, s3_recv, peers)
    for copy in spread:
        copy.start()
    for copy in spread:
        copy.wait()
    for j in range(n_plane):
        total[j * share:(j + 1) * share, :] = total_in[j]

    flat = jnp.concatenate([total[pl.ds(j, EXAMPLES, stride=BANK), :] for j in range(BANK)], axis=1)
    bank_rows = bank[...].reshape(BANK * 128, bank.shape[2])
    result = jnp.zeros(out_ref.shape, F32)
    for piece in split(flat, 3):
        result = result + jnp.dot(piece, bank_rows, preferred_element_type=F32)
    out_ref[...] = result * inverse


def on_device(n_ps, n_plane, n_tp, *args):
    x, g, down, up, m1a, m2a, m1b, m2b, seeds_a, seeds_b, segments, bank = args
    rows = x.shape[0]
    ra, rb = m1a.shape[1], m1b.shape[1]
    width = up_to(ra, 128) + up_to(rb, 128)
    inverse = 1.0 / math.sqrt((x.shape[1] + g.shape[1]) * n_tp * down.shape[1])
    share = EXAMPLES * BANK // n_plane
    any_spec = pl.BlockSpec(memory_space=pl.ANY)
    vmem = pl.BlockSpec(memory_space=pltpu.VMEM)
    n_chip = n_plane // 2
    plane_sem = pltpu.SemaphoreType.DMA((n_chip, 2))
    tp_sem = pltpu.SemaphoreType.DMA((n_tp - 1,))
    like = lambda a: pltpu.VMEM(a.shape, a.dtype)
    return pl.pallas_call(
        functools.partial(kernel, n_ps, n_plane, n_tp, inverse),
        out_shape=jax.ShapeDtypeStruct((EXAMPLES, bank.shape[2]), F32),
        in_specs=[any_spec] * 8 + [vmem] * 3 + [any_spec],
        out_specs=vmem,
        scratch_shapes=[
            like(x), like(g), like(down), like(up), like(m1a), like(m2a), like(m1b), like(m2b), like(bank),
            pltpu.VMEM((n_plane, rows, width), BF16),
            pltpu.VMEM((n_plane, rows, width), BF16),
            pltpu.VMEM((rows, 256), F32),
            pltpu.VMEM((n_tp - 1, rows // n_tp, 256), F32),
            pltpu.VMEM((rows // n_tp, 256), BF16),
            pltpu.VMEM((n_plane, rows, 256), BF16),
            pltpu.VMEM((n_plane, rows, 128), F32),
            pltpu.VMEM((width, EXAMPLES * 128), F32),
            pltpu.VMEM((n_plane, share, 128), F32),
            pltpu.VMEM((n_plane, share, 128), F32),
            pltpu.VMEM((share, 128), F32),
            pltpu.VMEM((n_tp, share, 128), F32),
            pltpu.VMEM((n_plane, share, 128), F32),
            pltpu.VMEM((EXAMPLES * BANK, 128), F32),
            pltpu.SemaphoreType.DMA((9,)),
            plane_sem, plane_sem, tp_sem, tp_sem, tp_sem, tp_sem, plane_sem, plane_sem,
            plane_sem, plane_sem, tp_sem, tp_sem, plane_sem, plane_sem,
        ],
        compiler_params=pltpu.CompilerParams(
            collective_id=0, has_side_effects=True, vmem_limit_bytes=48 * 1024 * 1024
        ),
    )(x, g, down, up, m1a, m2a, m1b, m2b, seeds_a, seeds_b, segments.reshape(n_plane, rows), bank)


def solution(mesh):
    n_ps, n_tp = mesh.shape["ps"], mesh.shape["tp"]
    n_plane = mesh.shape["ex"] * n_ps
    return jax.shard_map(
        functools.partial(on_device, n_ps, n_plane, n_tp),
        mesh=mesh,
        in_specs=(
            P(("ex", "ps"), "tp"),
            P(("ex", "ps"), "tp"),
            P("tp", None),
            P("tp", None),
            P("tp", ("ex", "ps"), None),
            P("tp", ("ex", "ps"), None),
            P("tp", ("ex", "ps"), None),
            P("tp", ("ex", "ps"), None),
            P("tp", ("ex", "ps")),
            P("tp", ("ex", "ps")),
            P(),
            P(None, None, ("ex", "tp", "ps")),
        ),
        out_specs=P(None, ("ex", "tp", "ps")),
        check_vma=False,
    )
```

```python
import functools
import math

import jax
import jax.numpy as jnp
from jax import lax
from jax.experimental import pallas as pl
from jax.experimental.pallas import tpu as pltpu
from jax.sharding import PartitionSpec as P

EXAMPLES = 4
BANK = 16
MESH = pl.DeviceIdType.MESH
F32 = jnp.float32
BF16 = jnp.bfloat16


def flip(index, mask):
    out, bit = index, 1
    while bit <= mask:
        if mask & bit:
            out = out + bit - 2 * bit * ((index // bit) % 2)
        bit *= 2
    return out


def up_to(value, step):
    return -(-value // step) * step


def contract_rows(left, right):
    return lax.dot_general(left, right, (((0,), (0,)), ((), ())), preferred_element_type=F32)


def split(value, parts):
    out = []
    for _ in range(parts):
        piece = value.astype(BF16)
        out.append(piece)
        value = value - piece.astype(F32)
    return out


def pieces_of(rb):
    blocks = -(-rb // 128)
    ends = [min(rb, 128 * -(-blocks * i // 3)) for i in range(4)]
    return [(lo, hi) for lo, hi in zip(ends[:-1], ends[1:]) if hi > lo]


def kernel(
    n_ps, n_plane, n_tp, inverse,
    x_hbm, g_hbm, down_hbm, up_hbm, m1a_hbm, m2a_hbm, m1b_hbm, m2b_hbm, seeds_a, seeds_b, segments, bank_hbm,
    out_ref,
    x, g, down, up, m1a, m2a, m1b, m2b, bank,
    stage_a, recv_a, stage_b, recv_b, part, part_in, rank_sum, ranks, picked_h, picked_u,
    sums, sums_in, mine, mine_in, total_in, total,
    load_sem, a_send, a_recv, b_send, b_recv, rs_send, rs_recv, ag_send, ag_recv, pl_send, pl_recv,
    s1_send, s1_recv, s2_send, s2_recv, s3_send, s3_recv,
):
    ex, tp, ps = lax.axis_index("ex"), lax.axis_index("tp"), lax.axis_index("ps")
    q = ex * n_ps + ps
    chip, core = q // 2, q % 2
    n_chip = n_plane // 2
    rows = x.shape[0]
    ra, rb = m1a.shape[1], m1b.shape[0]

    pairs = [(x_hbm, x), (g_hbm, g), (down_hbm, down), (up_hbm, up), (m1a_hbm, m1a), (m2a_hbm, m2a),
             (m1b_hbm.at[:, 0, :], m1b), (m2b_hbm.at[:, 0, :], m2b), (bank_hbm, bank)]
    loads = [pltpu.make_async_copy(a, b, load_sem.at[i]) for i, (a, b) in enumerate(pairs)]
    for i in (1, 0, 2, 3, 4, 5, 6, 7, 8):
        loads[i].start()

    def plane_id(peer):
        return {"ex": peer // n_ps, "ps": peer % n_ps}

    def tp_id(d):
        return {"tp": (tp + d) % n_tp}

    peers = [(mask, other) for mask in range(n_chip) for other in range(2) if mask or other]

    def peer_of(mask, other):
        return 2 * flip(chip, mask) + (core + other) % 2

    barrier = pltpu.get_barrier_semaphore()
    for mask, other in peers:
        pl.semaphore_signal(barrier, inc=1, device_id=plane_id(peer_of(mask, other)), device_id_type=MESH)
    for d in range(1, n_tp):
        pl.semaphore_signal(barrier, inc=1, device_id=tp_id(d), device_id_type=MESH)

    def plane_copies(src, dst, send, recv_sem, chosen):
        return [
            pltpu.make_async_remote_copy(
                src_ref=src(peer_of(mask, other)), dst_ref=dst, send_sem=send.at[mask, other],
                recv_sem=recv_sem.at[mask, other], device_id=plane_id(peer_of(mask, other)), device_id_type=MESH,
            )
            for mask, other in chosen
        ]

    loads[1].wait()
    spans = pieces_of(rb)
    b_copies = []
    for i, (lo, hi) in enumerate(spans):
        for j in range(n_plane):
            stage_b[j, lo:hi, :] = g[j * rb + lo:j * rb + hi, :]
        window = pl.ds(lo, up_to(hi, 16) - lo)
        b_copies.append(plane_copies(
            lambda peer: stage_b.at[peer, window], recv_b.at[q, window], b_send.at[i], b_recv.at[i], peers
        ))
        if i == 0:
            pl.semaphore_wait(barrier, n_plane - 1 + n_tp - 1)
        if i < len(spans) - 1:
            for copy in b_copies[i]:
                copy.start()

    loads[0].wait()
    loads[2].wait()
    loads[3].wait()
    part[:, 0:128] = jnp.dot(x[...], down[...], preferred_element_type=F32)
    part[:, 128:256] = contract_rows(g[...], up[...])
    slab = rows // n_tp

    def slab_at(t):
        return pl.ds(pl.multiple_of(t * slab, slab), slab)

    rs = [
        pltpu.make_async_remote_copy(
            src_ref=part.at[slab_at((tp + d) % n_tp)], dst_ref=part_in.at[d - 1], send_sem=rs_send.at[d - 1],
            recv_sem=rs_recv.at[d - 1], device_id=tp_id(d), device_id_type=MESH,
        )
        for d in range(1, n_tp)
    ]
    for copy in rs:
        copy.start()

    for j in range(n_plane):
        stage_a[j, :, 0:ra] = x[:, j * ra:(j + 1) * ra]
    a_copies = plane_copies(lambda peer: stage_a.at[peer], recv_a.at[q], a_send, a_recv, peers)
    recv_a[q] = stage_a[q]
    recv_b[q] = stage_b[q]
    seg = segments[...]
    inv_len = [1.0 / jnp.sum((seg == e).astype(F32), axis=(0, 1), keepdims=True) for e in range(EXAMPLES)]
    seg_t = jnp.transpose(seg.astype(F32))

    for copy in rs:
        copy.wait()
    summed = part[slab_at(tp), :]
    for d in range(1, n_tp):
        summed = summed + part_in[d - 1]
    rank_sum[...] = summed.astype(BF16)
    ranks[q, slab_at(tp), :] = rank_sum[...]
    ag = [
        pltpu.make_async_remote_copy(
            src_ref=rank_sum, dst_ref=ranks.at[q, slab_at(tp)], send_sem=ag_send.at[d - 1],
            recv_sem=ag_recv.at[d - 1], device_id=tp_id(d), device_id_type=MESH,
        )
        for d in range(1, n_tp)
    ]
    for copy in ag:
        copy.start()
    for copy in ag:
        copy.wait()

    far = plane_copies(lambda peer: ranks.at[q], ranks.at[q], pl_send, pl_recv, [(m, 0) for m in range(1, n_chip)])
    near = []
    for mask in range(n_chip):
        slot = ranks.at[2 * flip(chip, mask) + core]
        near += plane_copies(lambda peer: slot, slot, pl_send.at[pl.ds(mask, 1)], pl_recv.at[pl.ds(mask, 1)], [(0, 1)])
    for copy in far + near[:1] + a_copies + b_copies[-1]:
        copy.start()
    for arrived, onward in zip(far, near[1:]):
        arrived.wait()
        onward.start()
    for copy in near:
        copy.wait()

    for j in range(n_plane):
        both = ranks[j].astype(F32)
        label = jnp.broadcast_to(seg_t[:, j:j + 1], (rows, 256))
        for e in range(EXAMPLES):
            chosen = jnp.where(label == e, both, 0.0).astype(BF16)
            picked_h[j * rows:(j + 1) * rows, e * 128:(e + 1) * 128] = chosen[:, 0:128]
            picked_u[j * rows:(j + 1) * rows, e * 128:(e + 1) * 128] = chosen[:, 128:256]

    for load in loads[4:]:
        load.wait()
    bins = lax.broadcasted_iota(jnp.int32, (BANK, 128), 0)
    block_sums = [jnp.zeros((BANK, 128), F32) for _ in range(EXAMPLES)]

    def add_features(grads, m1, m2, seeds, size):
        first = 0.9 * m1
        second = 0.999 * m2
        select = (seeds == bins[:, :size]).astype(BF16)
        for e in range(EXAMPLES):
            grad = grads[:, e * 128:(e + 1) * 128] * inv_len[e]
            moved = first + 0.1 * grad
            scaled = second + 0.001 * grad * grad
            bottom = scaled * lax.rsqrt(scaled) + 1e-08
            guess = pl.reciprocal(bottom, approx=True)
            feature = moved * (guess * (2.0 - bottom * guess))
            for piece in split(feature, 2):
                block_sums[e] = block_sums[e] + jnp.dot(select, piece, preferred_element_type=F32)

    def up_rows(index):
        for copy in b_copies[index]:
            copy.wait()
        low, high = spans[index]
        for lo in range(low, high, 128):
            hi = min(lo + 128, high)
            block = jnp.concatenate([recv_b[j, lo:hi, :] for j in range(n_plane)], axis=1)
            grads = jnp.dot(block, picked_h[...], preferred_element_type=F32)
            add_features(grads, m1b[lo:hi, :], m2b[lo:hi, :], seeds_b[:, lo:hi], hi - lo)

    for index in range(len(spans) - 1):
        up_rows(index)
    for copy in a_copies:
        copy.wait()
    for lo in range(0, ra, 128):
        hi = min(lo + 128, ra)
        block = recv_a[:, :, lo:hi].reshape(n_plane * rows, hi - lo)
        grads = contract_rows(block, picked_u[...])
        add_features(grads, m1a[0, lo:hi, :], m2a[0, lo:hi, :], seeds_a[:, lo:hi], hi - lo)
    up_rows(len(spans) - 1)
    summed = block_sums

    share = sums.shape[1]
    every = jnp.concatenate(summed, axis=0)
    for j in range(n_plane):
        sums[j] = every[j * share:(j + 1) * share, :]
    scatter = plane_copies(lambda peer: sums.at[peer], sums_in.at[q], s1_send, s1_recv, peers)
    for copy in scatter:
        copy.start()
    sums_in[q] = sums[q]
    for copy in scatter:
        copy.wait()
    mine[...] = jnp.sum(sums_in[...], axis=0)
    cross = [
        pltpu.make_async_remote_copy(
            src_ref=mine, dst_ref=mine_in.at[tp], send_sem=s2_send.at[d - 1], recv_sem=s2_recv.at[d - 1],
            device_id=tp_id(d), device_id_type=MESH,
        )
        for d in range(1, n_tp)
    ]
    for copy in cross:
        copy.start()
    mine_in[tp] = mine[...]
    for copy in cross:
        copy.wait()
    total_in[q] = jnp.sum(mine_in[...], axis=0)
    spread = plane_copies(lambda peer: total_in.at[q], total_in.at[q], s3_send, s3_recv, peers)
    for copy in spread:
        copy.start()
    for copy in spread:
        copy.wait()
    for j in range(n_plane):
        total[j * share:(j + 1) * share, :] = total_in[j]

    flat = jnp.concatenate([total[pl.ds(j, EXAMPLES, stride=BANK), :] for j in range(BANK)], axis=1)
    bank_rows = bank[...].reshape(BANK * 128, bank.shape[2])
    high = flat.astype(BF16).astype(F32)
    both = jnp.concatenate([high, flat - high], axis=0).astype(BF16)
    result = jnp.dot(both, bank_rows, preferred_element_type=F32)
    out_ref[...] = (result[:EXAMPLES] + result[EXAMPLES:]) * inverse


def on_device(n_ps, n_plane, n_tp, *args):
    x, g, down, up, m1a, m2a, m1b, m2b, seeds_a, seeds_b, segments, bank = args
    rows = x.shape[0]
    ra, rb = m1a.shape[1], m1b.shape[1]
    pa, pb = up_to(ra, 128), up_to(rb, 16)
    g = g.T
    m1b, m2b = jnp.swapaxes(m1b, 0, 1), jnp.swapaxes(m2b, 0, 1)
    inverse = 1.0 / math.sqrt((x.shape[1] + g.shape[0]) * n_tp * down.shape[1])
    share = EXAMPLES * BANK // n_plane
    any_spec = pl.BlockSpec(memory_space=pltpu.HBM)
    vmem = pl.BlockSpec(memory_space=pltpu.VMEM)
    n_chip = n_plane // 2
    plane_sem = pltpu.SemaphoreType.DMA((n_chip, 2))
    piece_sem = pltpu.SemaphoreType.DMA((len(pieces_of(rb)), n_chip, 2))
    tp_sem = pltpu.SemaphoreType.DMA((n_tp - 1,))
    like = lambda a: pltpu.VMEM(a.shape, a.dtype)
    return pl.pallas_call(
        functools.partial(kernel, n_ps, n_plane, n_tp, inverse),
        out_shape=jax.ShapeDtypeStruct((EXAMPLES, bank.shape[2]), F32),
        in_specs=[any_spec] * 8 + [vmem] * 3 + [any_spec],
        out_specs=vmem,
        scratch_shapes=[
            like(x), like(g), like(down), like(up), like(m1a), like(m2a), pltpu.VMEM((rb, 128), F32), pltpu.VMEM((rb, 128), F32), like(bank),
            pltpu.VMEM((n_plane, rows, pa), BF16),
            pltpu.VMEM((n_plane, rows, pa), BF16),
            pltpu.VMEM((n_plane, pb, 128), BF16),
            pltpu.VMEM((n_plane, pb, 128), BF16),
            pltpu.VMEM((rows, 256), F32),
            pltpu.VMEM((n_tp - 1, rows // n_tp, 256), F32),
            pltpu.VMEM((rows // n_tp, 256), BF16),
            pltpu.VMEM((n_plane, rows, 256), BF16),
            pltpu.VMEM((n_plane * rows, EXAMPLES * 128), BF16),
            pltpu.VMEM((n_plane * rows, EXAMPLES * 128), BF16),
            pltpu.VMEM((n_plane, share, 128), F32),
            pltpu.VMEM((n_plane, share, 128), F32),
            pltpu.VMEM((share, 128), F32),
            pltpu.VMEM((n_tp, share, 128), F32),
            pltpu.VMEM((n_plane, share, 128), F32),
            pltpu.VMEM((EXAMPLES * BANK, 128), F32),
            pltpu.SemaphoreType.DMA((9,)),
            plane_sem, plane_sem, piece_sem, piece_sem, tp_sem, tp_sem, tp_sem, tp_sem, plane_sem, plane_sem,
            plane_sem, plane_sem, tp_sem, tp_sem, plane_sem, plane_sem,
        ],
        compiler_params=pltpu.CompilerParams(
            collective_id=0, has_side_effects=True, vmem_limit_bytes=63 * 1024 * 1024
        ),
    )(x, g, down, up, m1a, m2a, m1b, m2b, seeds_a, seeds_b, segments.reshape(n_plane, rows), bank)


def solution(mesh):
    n_ps, n_tp = mesh.shape["ps"], mesh.shape["tp"]
    n_plane = mesh.shape["ex"] * n_ps
    return jax.shard_map(
        functools.partial(on_device, n_ps, n_plane, n_tp),
        mesh=mesh,
        in_specs=(
            P(("ex", "ps"), "tp"),
            P(("ex", "ps"), "tp"),
            P("tp", None),
            P("tp", None),
            P("tp", ("ex", "ps"), None),
            P("tp", ("ex", "ps"), None),
            P("tp", ("ex", "ps"), None),
            P("tp", ("ex", "ps"), None),
            P("tp", ("ex", "ps")),
            P("tp", ("ex", "ps")),
            P(),
            P(None, None, ("ex", "tp", "ps")),
        ),
        out_specs=P(None, ("ex", "tp", "ps")),
        check_vma=False,
    )
```

```python
import functools
import math

import jax
import jax.numpy as jnp
from jax import lax
from jax.experimental import pallas as pl
from jax.experimental.pallas import tpu as pltpu
from jax.sharding import PartitionSpec as P

EXAMPLES = 4
BANK = 16
MESH = pl.DeviceIdType.MESH
F32 = jnp.float32
BF16 = jnp.bfloat16


def flip(index, mask):
    out, bit = index, 1
    while bit <= mask:
        if mask & bit:
            out = out + bit - 2 * bit * ((index // bit) % 2)
        bit *= 2
    return out


def up_to(value, step):
    return -(-value // step) * step


def contract_rows(left, right):
    return lax.dot_general(left, right, (((0,), (0,)), ((), ())), preferred_element_type=F32)


def split(value, parts):
    out = []
    for _ in range(parts):
        piece = value.astype(BF16)
        out.append(piece)
        value = value - piece.astype(F32)
    return out


def pieces_of(rb):
    blocks = -(-rb // 128)
    ends = [min(rb, 128 * -(-blocks * i // 3)) for i in range(4)]
    return [(lo, hi) for lo, hi in zip(ends[:-1], ends[1:]) if hi > lo]


def kernel(
    n_ps, n_plane, n_tp, inverse,
    x_hbm, g_hbm, down_hbm, up_hbm, m1a_hbm, m2a_hbm, m1b_hbm, m2b_hbm, seeds_a_hbm, seeds_b_hbm, segments_hbm,
    bank_hbm,
    out_ref,
    x, g, down, up, m1a, m2a, m1b, m2b, bank, seeds_a, seeds_b, segments,
    stage_a, recv_a, stage_b, recv_b, part, part_in, rank_sum, ranks, picked_h, picked_u,
    sums, sums_in, mine, mine_in, total_in, total,
    load_sem, a_send, a_recv, b_send, b_recv, rs_send, rs_recv, ag_send, ag_recv, pl_send, pl_recv,
    s1_send, s1_recv, s2_send, s2_recv, s3_send, s3_recv,
):
    ex, tp, ps = lax.axis_index("ex"), lax.axis_index("tp"), lax.axis_index("ps")
    q = ex * n_ps + ps
    chip, core = q // 2, q % 2
    n_chip = n_plane // 2
    rows = x.shape[0]
    ra, rb = m1a.shape[1], m1b.shape[0]

    pairs = [(x_hbm, x), (g_hbm, g), (down_hbm, down), (up_hbm, up), (m1a_hbm, m1a), (m2a_hbm, m2a),
             (m1b_hbm.at[:, 0, :], m1b), (m2b_hbm.at[:, 0, :], m2b), (bank_hbm, bank),
             (seeds_a_hbm, seeds_a), (seeds_b_hbm, seeds_b), (segments_hbm, segments)]
    loads = [pltpu.make_async_copy(a, b, load_sem.at[i]) for i, (a, b) in enumerate(pairs)]

    def plane_id(peer):
        return {"ex": peer // n_ps, "ps": peer % n_ps}

    def tp_id(d):
        return {"tp": (tp + d) % n_tp}

    peers = [(mask, other) for mask in range(n_chip) for other in range(2) if mask or other]

    def peer_of(mask, other):
        return 2 * flip(chip, mask) + (core + other) % 2

    barrier = pltpu.get_barrier_semaphore()
    for mask, other in peers:
        pl.semaphore_signal(barrier, inc=1, device_id=plane_id(peer_of(mask, other)), device_id_type=MESH)
    for d in range(1, n_tp):
        pl.semaphore_signal(barrier, inc=1, device_id=tp_id(d), device_id_type=MESH)
    for i in (1, 3, 0, 2, 11, 4, 5, 6, 7, 8, 9, 10):
        loads[i].start()

    def plane_copies(src, dst, send, recv_sem, chosen):
        return [
            pltpu.make_async_remote_copy(
                src_ref=src(peer_of(mask, other)), dst_ref=dst, send_sem=send.at[mask, other],
                recv_sem=recv_sem.at[mask, other], device_id=plane_id(peer_of(mask, other)), device_id_type=MESH,
            )
            for mask, other in chosen
        ]

    direct = ra % 128 == 0
    if direct:
        def columns(peer):
            return x_hbm.at[:, pl.ds(pl.multiple_of(peer * ra, ra), ra)]
        own = pltpu.make_async_copy(columns(q), recv_a.at[q], load_sem.at[len(loads)])
        own.start()
    else:
        loads[0].wait()
        for j in range(n_plane):
            stage_a[j, :, 0:ra] = x[:, j * ra:(j + 1) * ra]
        recv_a[q] = stage_a[q]
    a_copies = plane_copies(
        columns if direct else (lambda peer: stage_a.at[peer]), recv_a.at[q], a_send, a_recv, peers
    )
    pl.semaphore_wait(barrier, n_plane - 1 + n_tp - 1)
    for copy in a_copies:
        copy.start()

    loads[1].wait()
    loads[3].wait()
    part[:, 128:256] = contract_rows(g[...], up[...])
    if direct:
        loads[0].wait()
    loads[2].wait()
    part[:, 0:128] = jnp.dot(x[...], down[...], preferred_element_type=F32)
    slab = rows // n_tp

    def slab_at(t):
        return pl.ds(pl.multiple_of(t * slab, slab), slab)

    rs = [
        pltpu.make_async_remote_copy(
            src_ref=part.at[slab_at((tp + d) % n_tp)], dst_ref=part_in.at[d - 1], send_sem=rs_send.at[d - 1],
            recv_sem=rs_recv.at[d - 1], device_id=tp_id(d), device_id_type=MESH,
        )
        for d in range(1, n_tp)
    ]
    for copy in rs:
        copy.start()

    spans = pieces_of(rb)
    b_copies = []
    for i, (lo, hi) in enumerate(spans):
        for j in range(n_plane):
            stage_b[j, lo:hi, :] = g[j * rb + lo:j * rb + hi, :]
        window = pl.ds(lo, up_to(hi, 16) - lo)
        b_copies.append(plane_copies(
            lambda peer: stage_b.at[peer, window], recv_b.at[q, window], b_send.at[i], b_recv.at[i], peers
        ))
        if i == 0:
            for copy in b_copies[0]:
                copy.start()
    recv_b[q] = stage_b[q]
    loads[11].wait()
    seg = segments[...]
    inv_len = [1.0 / jnp.sum((seg == e).astype(F32), axis=(0, 1), keepdims=True) for e in range(EXAMPLES)]
    tenth = [0.1 * value for value in inv_len]
    small = [0.001 * value * value for value in inv_len]
    seg_t = jnp.transpose(seg.astype(F32))

    for copy in rs:
        copy.wait()
    summed = part[slab_at(tp), :]
    for d in range(1, n_tp):
        summed = summed + part_in[d - 1]
    rank_sum[...] = summed.astype(BF16)
    ranks[q, slab_at(tp), :] = rank_sum[...]
    ag = [
        pltpu.make_async_remote_copy(
            src_ref=rank_sum, dst_ref=ranks.at[q, slab_at(tp)], send_sem=ag_send.at[d - 1],
            recv_sem=ag_recv.at[d - 1], device_id=tp_id(d), device_id_type=MESH,
        )
        for d in range(1, n_tp)
    ]
    for copy in ag:
        copy.start()
    for copy in ag:
        copy.wait()

    far = plane_copies(lambda peer: ranks.at[q], ranks.at[q], pl_send, pl_recv, [(m, 0) for m in range(1, n_chip)])
    near = []
    for mask in range(n_chip):
        slot = ranks.at[2 * flip(chip, mask) + core]
        near += plane_copies(lambda peer: slot, slot, pl_send.at[pl.ds(mask, 1)], pl_recv.at[pl.ds(mask, 1)], [(0, 1)])
    for copy in far + near[:1] + [copy for piece in b_copies[1:] for copy in piece]:
        copy.start()
    for arrived, onward in zip(far, near[1:]):
        arrived.wait()
        onward.start()
    for copy in near:
        copy.wait()

    for j in range(n_plane):
        both = ranks[j].astype(F32)
        label = jnp.broadcast_to(seg_t[:, j:j + 1], (rows, 256))
        for e in range(EXAMPLES):
            chosen = jnp.where(label == e, both, 0.0).astype(BF16)
            picked_h[j * rows:(j + 1) * rows, e * 128:(e + 1) * 128] = chosen[:, 0:128]
            picked_u[j * rows:(j + 1) * rows, e * 128:(e + 1) * 128] = chosen[:, 128:256]

    for load in loads[4:11]:
        load.wait()
    bins = lax.broadcasted_iota(jnp.int32, (BANK, 128), 0)
    block_sums = [jnp.zeros((BANK, 128), F32) for _ in range(EXAMPLES)]

    def add_features(grads, m1, m2, seeds, size):
        first = 0.9 * m1
        second = 0.999 * m2
        select = (seeds == bins[:, :size]).astype(BF16)
        for e in range(EXAMPLES):
            grad = grads[:, e * 128:(e + 1) * 128]
            moved = first + tenth[e] * grad
            scaled = second + small[e] * (grad * grad)
            bottom = scaled * lax.rsqrt(scaled) + 1e-08
            guess = pl.reciprocal(bottom, approx=True)
            feature = moved * (guess * (2.0 - bottom * guess))
            for piece in split(feature, 2):
                block_sums[e] = block_sums[e] + jnp.dot(select, piece, preferred_element_type=F32)

    def up_rows(index):
        for copy in b_copies[index]:
            copy.wait()
        low, high = spans[index]
        for lo in range(low, high, 128):
            hi = min(lo + 128, high)
            block = jnp.concatenate([recv_b[j, lo:hi, :] for j in range(n_plane)], axis=1)
            grads = jnp.dot(block, picked_h[...], preferred_element_type=F32)
            add_features(grads, m1b[lo:hi, :], m2b[lo:hi, :], seeds_b[:, lo:hi], hi - lo)

    for copy in a_copies:
        copy.wait()
    if direct:
        own.wait()
    for lo in range(0, ra, 128):
        hi = min(lo + 128, ra)
        block = recv_a[:, :, lo:hi].reshape(n_plane * rows, hi - lo)
        grads = contract_rows(block, picked_u[...])
        add_features(grads, m1a[0, lo:hi, :], m2a[0, lo:hi, :], seeds_a[:, lo:hi], hi - lo)
    for index in range(len(spans)):
        up_rows(index)
    summed = block_sums

    share = sums.shape[1]
    every = jnp.concatenate(summed, axis=0)
    for j in range(n_plane):
        sums[j] = every[j * share:(j + 1) * share, :]
    scatter = plane_copies(lambda peer: sums.at[peer], sums_in.at[q], s1_send, s1_recv, peers)
    for copy in scatter:
        copy.start()
    sums_in[q] = sums[q]
    for copy in scatter:
        copy.wait()
    mine[...] = jnp.sum(sums_in[...], axis=0)
    cross = [
        pltpu.make_async_remote_copy(
            src_ref=mine, dst_ref=mine_in.at[tp], send_sem=s2_send.at[d - 1], recv_sem=s2_recv.at[d - 1],
            device_id=tp_id(d), device_id_type=MESH,
        )
        for d in range(1, n_tp)
    ]
    for copy in cross:
        copy.start()
    mine_in[tp] = mine[...]
    for copy in cross:
        copy.wait()
    total_in[q] = jnp.sum(mine_in[...], axis=0)
    spread = plane_copies(lambda peer: total_in.at[q], total_in.at[q], s3_send, s3_recv, peers)
    for copy in spread:
        copy.start()
    for copy in spread:
        copy.wait()
    for j in range(n_plane):
        total[j * share:(j + 1) * share, :] = total_in[j]

    flat = jnp.concatenate([total[pl.ds(j, EXAMPLES, stride=BANK), :] for j in range(BANK)], axis=1)
    bank_rows = bank[...].reshape(BANK * 128, bank.shape[2])
    high = flat.astype(BF16).astype(F32)
    both = jnp.concatenate([high, flat - high], axis=0).astype(BF16)
    result = jnp.dot(both, bank_rows, preferred_element_type=F32)
    out_ref[...] = (result[:EXAMPLES] + result[EXAMPLES:]) * inverse


def on_device(n_ps, n_plane, n_tp, *args):
    x, g, down, up, m1a, m2a, m1b, m2b, seeds_a, seeds_b, segments, bank = args
    rows = x.shape[0]
    ra, rb = m1a.shape[1], m1b.shape[1]
    pa, pb = up_to(ra, 128), up_to(rb, 16)
    g = g.T
    m1b, m2b = jnp.swapaxes(m1b, 0, 1), jnp.swapaxes(m2b, 0, 1)
    inverse = 1.0 / math.sqrt((x.shape[1] + g.shape[0]) * n_tp * down.shape[1])
    share = EXAMPLES * BANK // n_plane
    any_spec = pl.BlockSpec(memory_space=pltpu.HBM)
    vmem = pl.BlockSpec(memory_space=pltpu.VMEM)
    n_chip = n_plane // 2
    plane_sem = pltpu.SemaphoreType.DMA((n_chip, 2))
    piece_sem = pltpu.SemaphoreType.DMA((len(pieces_of(rb)), n_chip, 2))
    tp_sem = pltpu.SemaphoreType.DMA((n_tp - 1,))
    like = lambda a: pltpu.VMEM(a.shape, a.dtype)
    return pl.pallas_call(
        functools.partial(kernel, n_ps, n_plane, n_tp, inverse),
        out_shape=jax.ShapeDtypeStruct((EXAMPLES, bank.shape[2]), F32),
        in_specs=[any_spec] * 12,
        out_specs=vmem,
        scratch_shapes=[
            like(x), like(g), like(down), like(up), like(m1a), like(m2a), pltpu.VMEM((rb, 128), F32), pltpu.VMEM((rb, 128), F32), like(bank),
            like(seeds_a), like(seeds_b), pltpu.VMEM((n_plane, rows), jnp.int32),
            pltpu.VMEM((n_plane, rows, pa), BF16),
            pltpu.VMEM((n_plane, rows, pa), BF16),
            pltpu.VMEM((n_plane, pb, 128), BF16),
            pltpu.VMEM((n_plane, pb, 128), BF16),
            pltpu.VMEM((rows, 256), F32),
            pltpu.VMEM((n_tp - 1, rows // n_tp, 256), F32),
            pltpu.VMEM((rows // n_tp, 256), BF16),
            pltpu.VMEM((n_plane, rows, 256), BF16),
            pltpu.VMEM((n_plane * rows, EXAMPLES * 128), BF16),
            pltpu.VMEM((n_plane * rows, EXAMPLES * 128), BF16),
            pltpu.VMEM((n_plane, share, 128), F32),
            pltpu.VMEM((n_plane, share, 128), F32),
            pltpu.VMEM((share, 128), F32),
            pltpu.VMEM((n_tp, share, 128), F32),
            pltpu.VMEM((n_plane, share, 128), F32),
            pltpu.VMEM((EXAMPLES * BANK, 128), F32),
            pltpu.SemaphoreType.DMA((13,)),
            plane_sem, plane_sem, piece_sem, piece_sem, tp_sem, tp_sem, tp_sem, tp_sem, plane_sem, plane_sem,
            plane_sem, plane_sem, tp_sem, tp_sem, plane_sem, plane_sem,
        ],
        compiler_params=pltpu.CompilerParams(
            collective_id=0, has_side_effects=True, vmem_limit_bytes=63 * 1024 * 1024
        ),
    )(x, g, down, up, m1a, m2a, m1b, m2b, seeds_a, seeds_b, segments.reshape(n_plane, rows), bank)


def solution(mesh):
    n_ps, n_tp = mesh.shape["ps"], mesh.shape["tp"]
    n_plane = mesh.shape["ex"] * n_ps
    return jax.shard_map(
        functools.partial(on_device, n_ps, n_plane, n_tp),
        mesh=mesh,
        in_specs=(
            P(("ex", "ps"), "tp"),
            P(("ex", "ps"), "tp"),
            P("tp", None),
            P("tp", None),
            P("tp", ("ex", "ps"), None),
            P("tp", ("ex", "ps"), None),
            P("tp", ("ex", "ps"), None),
            P("tp", ("ex", "ps"), None),
            P("tp", ("ex", "ps")),
            P("tp", ("ex", "ps")),
            P(),
            P(None, None, ("ex", "tp", "ps")),
        ),
        out_specs=P(None, ("ex", "tp", "ps")),
        check_vma=False,
    )
```

```python
import functools
import math

import jax
import jax.numpy as jnp
from jax import lax
from jax.experimental import pallas as pl
from jax.experimental.pallas import tpu as pltpu
from jax.sharding import PartitionSpec as P

EXAMPLES = 4
BANK = 16
MESH = pl.DeviceIdType.MESH
F32 = jnp.float32
BF16 = jnp.bfloat16


def flip(index, mask):
    out, bit = index, 1
    while bit <= mask:
        if mask & bit:
            out = out + bit - 2 * bit * ((index // bit) % 2)
        bit *= 2
    return out


def up_to(value, step):
    return -(-value // step) * step


def contract_rows(left, right):
    return lax.dot_general(left, right, (((0,), (0,)), ((), ())), preferred_element_type=F32)


def split(value, parts):
    out = []
    for _ in range(parts):
        piece = value.astype(BF16)
        out.append(piece)
        value = value - piece.astype(F32)
    return out


def pieces_of(rb):
    blocks = -(-rb // 128)
    ends = [min(rb, 128 * -(-blocks * i // 3)) for i in range(4)]
    return [(lo, hi) for lo, hi in zip(ends[:-1], ends[1:]) if hi > lo]


def kernel(
    n_ps, n_plane, n_tp, inverse,
    x_hbm, g_hbm, down_hbm, up_hbm, m1a_hbm, m2a_hbm, m1b_hbm, m2b_hbm, seeds_a_hbm, seeds_b_hbm, segments_hbm,
    bank_hbm,
    out_ref,
    x, g, down, up, m1a, m2a, m1b, m2b, bank, seeds_a, seeds_b, segments,
    stage_a, recv_a, stage_b, recv_b, part, part_in, rank_sum, ranks, picked_h, picked_u,
    sums, sums_in, mine, mine_in, total_in, total,
    load_sem, a_send, a_recv, b_send, b_recv, rs_send, rs_recv, ag_send, ag_recv, pl_send, pl_recv,
    s1_send, s1_recv, s2_send, s2_recv, s3_send, s3_recv,
):
    ex, tp, ps = lax.axis_index("ex"), lax.axis_index("tp"), lax.axis_index("ps")
    q = ex * n_ps + ps
    chip, core = q // 2, q % 2
    n_chip = n_plane // 2
    rows = x.shape[0]
    ra, rb = m1a.shape[1], m1b.shape[0]

    pairs = [(x_hbm, x), (g_hbm, g), (down_hbm, down), (up_hbm, up), (m1a_hbm, m1a), (m2a_hbm, m2a),
             (m1b_hbm.at[:, 0, :], m1b), (m2b_hbm.at[:, 0, :], m2b), (bank_hbm, bank),
             (seeds_a_hbm, seeds_a), (seeds_b_hbm, seeds_b), (segments_hbm, segments)]
    loads = [pltpu.make_async_copy(a, b, load_sem.at[i]) for i, (a, b) in enumerate(pairs)]

    def plane_id(peer):
        return {"ex": peer // n_ps, "ps": peer % n_ps}

    def tp_id(d):
        return {"tp": (tp + d) % n_tp}

    peers = [(mask, other) for mask in range(n_chip) for other in range(2) if mask or other]

    def peer_of(mask, other):
        return 2 * flip(chip, mask) + (core + other) % 2

    barrier = pltpu.get_barrier_semaphore()
    for mask, other in peers:
        pl.semaphore_signal(barrier, inc=1, device_id=plane_id(peer_of(mask, other)), device_id_type=MESH)
    for d in range(1, n_tp):
        pl.semaphore_signal(barrier, inc=1, device_id=tp_id(d), device_id_type=MESH)
    for i in (1, 3, 0, 2, 11, 4, 5, 6, 7, 8, 9, 10):
        loads[i].start()

    def plane_copies(src, dst, send, recv_sem, chosen):
        return [
            pltpu.make_async_remote_copy(
                src_ref=src(peer_of(mask, other)), dst_ref=dst, send_sem=send.at[mask, other],
                recv_sem=recv_sem.at[mask, other], device_id=plane_id(peer_of(mask, other)), device_id_type=MESH,
            )
            for mask, other in chosen
        ]

    direct = ra % 128 == 0
    if direct:
        def columns(peer):
            return x_hbm.at[:, pl.ds(pl.multiple_of(peer * ra, ra), ra)]
        own = pltpu.make_async_copy(columns(q), recv_a.at[q], load_sem.at[len(loads)])
        own.start()
    else:
        loads[0].wait()
        for j in range(n_plane):
            stage_a[j, :, 0:ra] = x[:, j * ra:(j + 1) * ra]
        recv_a[q] = stage_a[q]
    a_copies = plane_copies(
        columns if direct else (lambda peer: stage_a.at[peer]), recv_a.at[q], a_send, a_recv, peers
    )
    pl.semaphore_wait(barrier, n_plane - 1 + n_tp - 1)
    for copy in a_copies:
        copy.start()

    loads[1].wait()
    loads[3].wait()
    part[:, 128:256] = contract_rows(g[...], up[...])
    if direct:
        loads[0].wait()
    loads[2].wait()
    part[:, 0:128] = jnp.dot(x[...], down[...], preferred_element_type=F32)
    slab = rows // n_tp

    def slab_at(t):
        return pl.ds(pl.multiple_of(t * slab, slab), slab)

    rs = [
        pltpu.make_async_remote_copy(
            src_ref=part.at[slab_at((tp + d) % n_tp)], dst_ref=part_in.at[d - 1], send_sem=rs_send.at[d - 1],
            recv_sem=rs_recv.at[d - 1], device_id=tp_id(d), device_id_type=MESH,
        )
        for d in range(1, n_tp)
    ]
    for copy in rs:
        copy.start()

    spans = pieces_of(rb)
    b_copies = []
    for i, (lo, hi) in enumerate(spans):
        for j in range(n_plane):
            stage_b[j, lo:hi, :] = g[j * rb + lo:j * rb + hi, :]
        window = pl.ds(lo, up_to(hi, 16) - lo)
        b_copies.append(plane_copies(
            lambda peer: stage_b.at[peer, window], recv_b.at[q, window], b_send.at[i], b_recv.at[i], peers
        ))
        if i == 0:
            for copy in b_copies[0]:
                copy.start()
    recv_b[q] = stage_b[q]
    loads[11].wait()
    seg = segments[...]
    inv_len = [1.0 / jnp.sum((seg == e).astype(F32), axis=(0, 1), keepdims=True) for e in range(EXAMPLES)]
    tenth = [0.1 * value for value in inv_len]
    small = [0.001 * value * value for value in inv_len]
    seg_t = jnp.transpose(seg.astype(F32))

    for copy in rs:
        copy.wait()
    summed = part[slab_at(tp), :]
    for d in range(1, n_tp):
        summed = summed + part_in[d - 1]
    rank_sum[...] = summed.astype(BF16)
    ranks[q, slab_at(tp), :] = rank_sum[...]
    ag = [
        pltpu.make_async_remote_copy(
            src_ref=rank_sum, dst_ref=ranks.at[q, slab_at(tp)], send_sem=ag_send.at[d - 1],
            recv_sem=ag_recv.at[d - 1], device_id=tp_id(d), device_id_type=MESH,
        )
        for d in range(1, n_tp)
    ]
    for copy in ag:
        copy.start()
    for copy in ag:
        copy.wait()

    far = plane_copies(lambda peer: ranks.at[q], ranks.at[q], pl_send, pl_recv, [(m, 0) for m in range(1, n_chip)])
    near = []
    for mask in range(n_chip):
        slot = ranks.at[2 * flip(chip, mask) + core]
        near += plane_copies(lambda peer: slot, slot, pl_send.at[pl.ds(mask, 1)], pl_recv.at[pl.ds(mask, 1)], [(0, 1)])
    for copy in far + near[:1] + [copy for piece in b_copies[1:] for copy in piece]:
        copy.start()
    for arrived, onward in zip(far, near[1:]):
        arrived.wait()
        onward.start()
    for copy in near:
        copy.wait()

    for j in range(n_plane):
        both = ranks[j].astype(F32)
        label = jnp.broadcast_to(seg_t[:, j:j + 1], (rows, 256))
        for e in range(EXAMPLES):
            chosen = jnp.where(label == e, both, 0.0).astype(BF16)
            picked_h[j * rows:(j + 1) * rows, e * 128:(e + 1) * 128] = chosen[:, 0:128]
            picked_u[j * rows:(j + 1) * rows, e * 128:(e + 1) * 128] = chosen[:, 128:256]

    for load in loads[4:11]:
        load.wait()
    bins = lax.broadcasted_iota(jnp.int32, (BANK, 128), 0)
    block_sums = jnp.zeros((BANK, EXAMPLES * 128), F32)

    def add_features(block_sums, grads, m1, m2, seeds, size):
        first = 0.9 * m1
        second = 0.999 * m2
        select = (seeds == bins[:, :size]).astype(BF16)
        features = []
        for e in range(EXAMPLES):
            grad = grads[:, e * 128:(e + 1) * 128]
            moved = first + tenth[e] * grad
            scaled = second + small[e] * (grad * grad)
            bottom = scaled * lax.rsqrt(scaled) + 1e-08
            guess = pl.reciprocal(bottom, approx=True)
            features.append(split(moved * (guess * (2.0 - bottom * guess)), 2))
        high, low = (jnp.concatenate([feature[i] for feature in features], axis=1) for i in range(2))
        if size == 128:
            twice = jnp.concatenate([select, select], axis=1)
            return block_sums + jnp.dot(twice, jnp.concatenate([high, low], axis=0), preferred_element_type=F32)
        block_sums = block_sums + jnp.dot(select, high, preferred_element_type=F32)
        return block_sums + jnp.dot(select, low, preferred_element_type=F32)

    for copy in a_copies:
        copy.wait()
    if direct:
        own.wait()
    block = recv_a[:, :, 0:ra].reshape(n_plane * rows, ra)
    grads = contract_rows(block, picked_u[...])
    for lo in range(0, ra, 128):
        hi = min(lo + 128, ra)
        block_sums = add_features(
            block_sums, grads[lo:hi], m1a[0, lo:hi, :], m2a[0, lo:hi, :], seeds_a[:, lo:hi], hi - lo
        )
    for (low, high), copies in zip(spans, b_copies):
        for copy in copies:
            copy.wait()
        block = jnp.concatenate([recv_b[j, low:high, :] for j in range(n_plane)], axis=1)
        grads = jnp.dot(block, picked_h[...], preferred_element_type=F32)
        for lo in range(low, high, 128):
            hi = min(lo + 128, high)
            block_sums = add_features(
                block_sums, grads[lo - low:hi - low], m1b[lo:hi, :], m2b[lo:hi, :], seeds_b[:, lo:hi], hi - lo
            )
    summed = [block_sums[:, e * 128:(e + 1) * 128] for e in range(EXAMPLES)]

    share = sums.shape[1]
    every = jnp.concatenate(summed, axis=0)
    for j in range(n_plane):
        sums[j] = every[j * share:(j + 1) * share, :]
    scatter = plane_copies(lambda peer: sums.at[peer], sums_in.at[q], s1_send, s1_recv, peers)
    for copy in scatter:
        copy.start()
    sums_in[q] = sums[q]
    for copy in scatter:
        copy.wait()
    mine[...] = jnp.sum(sums_in[...], axis=0)
    cross = [
        pltpu.make_async_remote_copy(
            src_ref=mine, dst_ref=mine_in.at[tp], send_sem=s2_send.at[d - 1], recv_sem=s2_recv.at[d - 1],
            device_id=tp_id(d), device_id_type=MESH,
        )
        for d in range(1, n_tp)
    ]
    for copy in cross:
        copy.start()
    mine_in[tp] = mine[...]
    for copy in cross:
        copy.wait()
    total_in[q] = jnp.sum(mine_in[...], axis=0)
    spread = plane_copies(lambda peer: total_in.at[q], total_in.at[q], s3_send, s3_recv, peers)
    for copy in spread:
        copy.start()
    for copy in spread:
        copy.wait()
    for j in range(n_plane):
        total[j * share:(j + 1) * share, :] = total_in[j]

    flat = jnp.concatenate([total[pl.ds(j, EXAMPLES, stride=BANK), :] for j in range(BANK)], axis=1)
    bank_rows = bank[...].reshape(BANK * 128, bank.shape[2])
    high = flat.astype(BF16).astype(F32)
    both = jnp.concatenate([high, flat - high], axis=0).astype(BF16)
    result = jnp.dot(both, bank_rows, preferred_element_type=F32)
    out_ref[...] = (result[:EXAMPLES] + result[EXAMPLES:]) * inverse


def on_device(n_ps, n_plane, n_tp, *args):
    x, g, down, up, m1a, m2a, m1b, m2b, seeds_a, seeds_b, segments, bank = args
    rows = x.shape[0]
    ra, rb = m1a.shape[1], m1b.shape[1]
    pa, pb = up_to(ra, 128), up_to(rb, 16)
    g = g.T
    m1b, m2b = jnp.swapaxes(m1b, 0, 1), jnp.swapaxes(m2b, 0, 1)
    inverse = 1.0 / math.sqrt((x.shape[1] + g.shape[0]) * n_tp * down.shape[1])
    share = EXAMPLES * BANK // n_plane
    any_spec = pl.BlockSpec(memory_space=pltpu.HBM)
    vmem = pl.BlockSpec(memory_space=pltpu.VMEM)
    n_chip = n_plane // 2
    plane_sem = pltpu.SemaphoreType.DMA((n_chip, 2))
    piece_sem = pltpu.SemaphoreType.DMA((len(pieces_of(rb)), n_chip, 2))
    tp_sem = pltpu.SemaphoreType.DMA((n_tp - 1,))
    like = lambda a: pltpu.VMEM(a.shape, a.dtype)
    return pl.pallas_call(
        functools.partial(kernel, n_ps, n_plane, n_tp, inverse),
        out_shape=jax.ShapeDtypeStruct((EXAMPLES, bank.shape[2]), F32),
        in_specs=[any_spec] * 12,
        out_specs=vmem,
        scratch_shapes=[
            like(x), like(g), like(down), like(up), like(m1a), like(m2a), pltpu.VMEM((rb, 128), F32), pltpu.VMEM((rb, 128), F32), like(bank),
            like(seeds_a), like(seeds_b), pltpu.VMEM((n_plane, rows), jnp.int32),
            pltpu.VMEM((n_plane, rows, pa), BF16),
            pltpu.VMEM((n_plane, rows, pa), BF16),
            pltpu.VMEM((n_plane, pb, 128), BF16),
            pltpu.VMEM((n_plane, pb, 128), BF16),
            pltpu.VMEM((rows, 256), F32),
            pltpu.VMEM((n_tp - 1, rows // n_tp, 256), F32),
            pltpu.VMEM((rows // n_tp, 256), BF16),
            pltpu.VMEM((n_plane, rows, 256), BF16),
            pltpu.VMEM((n_plane * rows, EXAMPLES * 128), BF16),
            pltpu.VMEM((n_plane * rows, EXAMPLES * 128), BF16),
            pltpu.VMEM((n_plane, share, 128), F32),
            pltpu.VMEM((n_plane, share, 128), F32),
            pltpu.VMEM((share, 128), F32),
            pltpu.VMEM((n_tp, share, 128), F32),
            pltpu.VMEM((n_plane, share, 128), F32),
            pltpu.VMEM((EXAMPLES * BANK, 128), F32),
            pltpu.SemaphoreType.DMA((13,)),
            plane_sem, plane_sem, piece_sem, piece_sem, tp_sem, tp_sem, tp_sem, tp_sem, plane_sem, plane_sem,
            plane_sem, plane_sem, tp_sem, tp_sem, plane_sem, plane_sem,
        ],
        compiler_params=pltpu.CompilerParams(
            collective_id=0, has_side_effects=True, vmem_limit_bytes=63 * 1024 * 1024
        ),
    )(x, g, down, up, m1a, m2a, m1b, m2b, seeds_a, seeds_b, segments.reshape(n_plane, rows), bank)


def solution(mesh):
    n_ps, n_tp = mesh.shape["ps"], mesh.shape["tp"]
    n_plane = mesh.shape["ex"] * n_ps
    return jax.shard_map(
        functools.partial(on_device, n_ps, n_plane, n_tp),
        mesh=mesh,
        in_specs=(
            P(("ex", "ps"), "tp"),
            P(("ex", "ps"), "tp"),
            P("tp", None),
            P("tp", None),
            P("tp", ("ex", "ps"), None),
            P("tp", ("ex", "ps"), None),
            P("tp", ("ex", "ps"), None),
            P("tp", ("ex", "ps"), None),
            P("tp", ("ex", "ps")),
            P("tp", ("ex", "ps")),
            P(),
            P(None, None, ("ex", "tp", "ps")),
        ),
        out_specs=P(None, ("ex", "tp", "ps")),
        check_vma=False,
    )
```

```python
import functools
import math

import jax
import jax.numpy as jnp
from jax import lax
from jax.experimental import pallas as pl
from jax.experimental.pallas import tpu as pltpu
from jax.sharding import PartitionSpec as P

EXAMPLES = 4
BANK = 16
MESH = pl.DeviceIdType.MESH
F32 = jnp.float32
BF16 = jnp.bfloat16


def flip(index, mask):
    out, bit = index, 1
    while bit <= mask:
        if mask & bit:
            out = out + bit - 2 * bit * ((index // bit) % 2)
        bit *= 2
    return out


def up_to(value, step):
    return -(-value // step) * step


def contract_rows(left, right):
    return lax.dot_general(left, right, (((0,), (0,)), ((), ())), preferred_element_type=F32)


def split(value, parts):
    out = []
    for _ in range(parts):
        piece = value.astype(BF16)
        out.append(piece)
        value = value - piece.astype(F32)
    return out


def pieces_of(rb):
    blocks = -(-rb // 128)
    ends = [min(rb, 128 * -(-blocks * i // 4)) for i in range(5)]
    return [(lo, hi) for lo, hi in zip(ends[:-1], ends[1:]) if hi > lo]


def kernel(
    n_ps, n_plane, n_tp, inverse,
    x_hbm, g_hbm, down_hbm, up_hbm, m1a_hbm, m2a_hbm, m1b_hbm, m2b_hbm, seeds_a_hbm, seeds_b_hbm, segments_hbm,
    bank_hbm,
    out_ref,
    x, g, down, up, m1a, m2a, m1b, m2b, bank, seeds_a, seeds_b, segments,
    stage_a, recv_a, stage_b, recv_b, part, part_in, rank_sum, ranks, picked_h, picked_u,
    sums, sums_in, mine, mine_in, total_in, total,
    load_sem, a_send, a_recv, b_send, b_recv, rs_send, rs_recv, ag_send, ag_recv, pl_send, pl_recv,
    s1_send, s1_recv, s2_send, s2_recv, s3_send, s3_recv,
):
    ex, tp, ps = lax.axis_index("ex"), lax.axis_index("tp"), lax.axis_index("ps")
    q = ex * n_ps + ps
    chip, core = q // 2, q % 2
    n_chip = n_plane // 2
    rows = x.shape[0]
    ra, rb = m1a.shape[1], m1b.shape[0]

    pairs = [(x_hbm, x), (g_hbm, g), (down_hbm, down), (up_hbm, up), (m1a_hbm, m1a), (m2a_hbm, m2a),
             (m1b_hbm.at[:, 0, :], m1b), (m2b_hbm.at[:, 0, :], m2b), (bank_hbm, bank),
             (seeds_a_hbm, seeds_a), (seeds_b_hbm, seeds_b), (segments_hbm, segments)]
    loads = [pltpu.make_async_copy(a, b, load_sem.at[i]) for i, (a, b) in enumerate(pairs)]

    def plane_id(peer):
        return {"ex": peer // n_ps, "ps": peer % n_ps}

    def tp_id(d):
        return {"tp": (tp + d) % n_tp}

    peers = [(mask, other) for mask in range(n_chip) for other in range(2) if mask or other]

    def peer_of(mask, other):
        return 2 * flip(chip, mask) + (core + other) % 2

    barrier = pltpu.get_barrier_semaphore()
    for mask, other in peers:
        pl.semaphore_signal(barrier, inc=1, device_id=plane_id(peer_of(mask, other)), device_id_type=MESH)
    for d in range(1, n_tp):
        pl.semaphore_signal(barrier, inc=1, device_id=tp_id(d), device_id_type=MESH)
    for i in (1, 3, 0, 2, 11, 4, 5, 6, 7, 8, 9, 10):
        loads[i].start()

    def plane_copies(src, dst, send, recv_sem, chosen):
        return [
            pltpu.make_async_remote_copy(
                src_ref=src(peer_of(mask, other)), dst_ref=dst, send_sem=send.at[mask, other],
                recv_sem=recv_sem.at[mask, other], device_id=plane_id(peer_of(mask, other)), device_id_type=MESH,
            )
            for mask, other in chosen
        ]

    direct = ra % 128 == 0
    if direct:
        def columns(peer):
            return x_hbm.at[:, pl.ds(pl.multiple_of(peer * ra, ra), ra)]
        own = pltpu.make_async_copy(columns(q), recv_a.at[q], load_sem.at[len(loads)])
        own.start()
    else:
        loads[0].wait()
        for j in range(n_plane):
            stage_a[j, :, 0:ra] = x[:, j * ra:(j + 1) * ra]
        recv_a[q] = stage_a[q]
    a_copies = plane_copies(
        columns if direct else (lambda peer: stage_a.at[peer]), recv_a.at[q], a_send, a_recv, peers
    )
    pl.semaphore_wait(barrier, n_plane - 1 + n_tp - 1)
    for copy in a_copies:
        copy.start()

    loads[1].wait()
    loads[3].wait()
    part[:, 128:256] = contract_rows(g[...], up[...])
    if direct:
        loads[0].wait()
    loads[2].wait()
    part[:, 0:128] = jnp.dot(x[...], down[...], preferred_element_type=F32)
    slab = rows // n_tp

    def slab_at(t):
        return pl.ds(pl.multiple_of(t * slab, slab), slab)

    rs = [
        pltpu.make_async_remote_copy(
            src_ref=part.at[slab_at((tp + d) % n_tp)], dst_ref=part_in.at[d - 1], send_sem=rs_send.at[d - 1],
            recv_sem=rs_recv.at[d - 1], device_id=tp_id(d), device_id_type=MESH,
        )
        for d in range(1, n_tp)
    ]
    for copy in rs:
        copy.start()

    spans = pieces_of(rb)
    b_copies = []
    for i, (lo, hi) in enumerate(spans):
        for j in range(n_plane):
            stage_b[j, lo:hi, :] = g[j * rb + lo:j * rb + hi, :]
        window = pl.ds(lo, up_to(hi, 16) - lo)
        b_copies.append(plane_copies(
            lambda peer: stage_b.at[peer, window], recv_b.at[q, window], b_send.at[i], b_recv.at[i], peers
        ))
        if i == 0:
            for copy in b_copies[0]:
                copy.start()
    recv_b[q] = stage_b[q]
    loads[11].wait()
    seg = segments[...]
    inv_len = [1.0 / jnp.sum((seg == e).astype(F32), axis=(0, 1), keepdims=True) for e in range(EXAMPLES)]
    tenth = [0.1 * value for value in inv_len]
    small = [0.001 * value * value for value in inv_len]
    seg_t = jnp.transpose(seg.astype(F32))

    for copy in rs:
        copy.wait()
    summed = part[slab_at(tp), :]
    for d in range(1, n_tp):
        summed = summed + part_in[d - 1]
    rank_sum[...] = summed.astype(BF16)
    ranks[q, slab_at(tp), :] = rank_sum[...]
    ag = [
        pltpu.make_async_remote_copy(
            src_ref=rank_sum, dst_ref=ranks.at[q, slab_at(tp)], send_sem=ag_send.at[d - 1],
            recv_sem=ag_recv.at[d - 1], device_id=tp_id(d), device_id_type=MESH,
        )
        for d in range(1, n_tp)
    ]
    for copy in ag:
        copy.start()
    for copy in ag:
        copy.wait()

    far = plane_copies(lambda peer: ranks.at[q], ranks.at[q], pl_send, pl_recv, [(m, 0) for m in range(1, n_chip)])
    near = []
    for mask in range(n_chip):
        slot = ranks.at[2 * flip(chip, mask) + core]
        near += plane_copies(lambda peer: slot, slot, pl_send.at[pl.ds(mask, 1)], pl_recv.at[pl.ds(mask, 1)], [(0, 1)])
    for copy in far + near[:1] + [copy for piece in b_copies[1:] for copy in piece]:
        copy.start()
    for arrived, onward in zip(far, near[1:]):
        arrived.wait()
        onward.start()
    for copy in near:
        copy.wait()

    for j in range(n_plane):
        both = ranks[j].astype(F32)
        label = jnp.broadcast_to(seg_t[:, j:j + 1], (rows, 256))
        for e in range(EXAMPLES):
            chosen = jnp.where(label == e, both, 0.0).astype(BF16)
            picked_h[j * rows:(j + 1) * rows, e * 128:(e + 1) * 128] = chosen[:, 0:128]
            picked_u[j * rows:(j + 1) * rows, e * 128:(e + 1) * 128] = chosen[:, 128:256]

    for load in loads[4:11]:
        load.wait()
    bins = lax.broadcasted_iota(jnp.int32, (BANK, 128), 0)
    block_sums = jnp.zeros((BANK, EXAMPLES * 128), F32)

    def add_features(block_sums, grads, m1, m2, seeds, size):
        first = 0.9 * m1
        second = 0.999 * m2
        select = (seeds == bins[:, :size]).astype(BF16)
        features = []
        for e in range(EXAMPLES):
            grad = grads[:, e * 128:(e + 1) * 128]
            moved = first + tenth[e] * grad
            scaled = second + small[e] * (grad * grad)
            bottom = scaled * lax.rsqrt(scaled) + 1e-08
            guess = pl.reciprocal(bottom, approx=True)
            features.append(split(moved * (guess * (2.0 - bottom * guess)), 2))
        high, low = (jnp.concatenate([feature[i] for feature in features], axis=1) for i in range(2))
        if size == 128:
            twice = jnp.concatenate([select, select], axis=1)
            return block_sums + jnp.dot(twice, jnp.concatenate([high, low], axis=0), preferred_element_type=F32)
        block_sums = block_sums + jnp.dot(select, high, preferred_element_type=F32)
        return block_sums + jnp.dot(select, low, preferred_element_type=F32)

    for copy in a_copies:
        copy.wait()
    if direct:
        own.wait()
    block = recv_a[:, :, 0:ra].reshape(n_plane * rows, ra)
    grads = contract_rows(block, picked_u[...])
    for lo in range(0, ra, 128):
        hi = min(lo + 128, ra)
        block_sums = add_features(
            block_sums, grads[lo:hi], m1a[0, lo:hi, :], m2a[0, lo:hi, :], seeds_a[:, lo:hi], hi - lo
        )
    for (low, high), copies in zip(spans, b_copies):
        for copy in copies:
            copy.wait()
        block = jnp.concatenate([recv_b[j, low:high, :] for j in range(n_plane)], axis=1)
        grads = jnp.dot(block, picked_h[...], preferred_element_type=F32)
        for lo in range(low, high, 128):
            hi = min(lo + 128, high)
            block_sums = add_features(
                block_sums, grads[lo - low:hi - low], m1b[lo:hi, :], m2b[lo:hi, :], seeds_b[:, lo:hi], hi - lo
            )
    summed = [block_sums[:, e * 128:(e + 1) * 128] for e in range(EXAMPLES)]

    share = sums.shape[1]
    every = jnp.concatenate(summed, axis=0)
    for j in range(n_plane):
        sums[j] = every[j * share:(j + 1) * share, :]
    scatter = plane_copies(lambda peer: sums.at[peer], sums_in.at[q], s1_send, s1_recv, peers)
    for copy in scatter:
        copy.start()
    sums_in[q] = sums[q]
    for copy in scatter:
        copy.wait()
    mine[...] = jnp.sum(sums_in[...], axis=0)
    cross = [
        pltpu.make_async_remote_copy(
            src_ref=mine, dst_ref=mine_in.at[tp], send_sem=s2_send.at[d - 1], recv_sem=s2_recv.at[d - 1],
            device_id=tp_id(d), device_id_type=MESH,
        )
        for d in range(1, n_tp)
    ]
    for copy in cross:
        copy.start()
    mine_in[tp] = mine[...]
    for copy in cross:
        copy.wait()
    total_in[q] = jnp.sum(mine_in[...], axis=0)
    spread = plane_copies(lambda peer: total_in.at[q], total_in.at[q], s3_send, s3_recv, peers)
    for copy in spread:
        copy.start()
    for copy in spread:
        copy.wait()
    for j in range(n_plane):
        total[j * share:(j + 1) * share, :] = total_in[j]

    flat = jnp.concatenate([total[pl.ds(j, EXAMPLES, stride=BANK), :] for j in range(BANK)], axis=1)
    bank_rows = bank[...].reshape(BANK * 128, bank.shape[2])
    high = flat.astype(BF16).astype(F32)
    both = jnp.concatenate([high, flat - high], axis=0).astype(BF16)
    result = jnp.dot(both, bank_rows, preferred_element_type=F32)
    out_ref[...] = (result[:EXAMPLES] + result[EXAMPLES:]) * inverse


def on_device(n_ps, n_plane, n_tp, *args):
    x, g, down, up, m1a, m2a, m1b, m2b, seeds_a, seeds_b, segments, bank = args
    rows = x.shape[0]
    ra, rb = m1a.shape[1], m1b.shape[1]
    pa, pb = up_to(ra, 128), up_to(rb, 16)
    g = g.T
    m1b, m2b = jnp.swapaxes(m1b, 0, 1), jnp.swapaxes(m2b, 0, 1)
    inverse = 1.0 / math.sqrt((x.shape[1] + g.shape[0]) * n_tp * down.shape[1])
    share = EXAMPLES * BANK // n_plane
    any_spec = pl.BlockSpec(memory_space=pltpu.HBM)
    vmem = pl.BlockSpec(memory_space=pltpu.VMEM)
    n_chip = n_plane // 2
    plane_sem = pltpu.SemaphoreType.DMA((n_chip, 2))
    piece_sem = pltpu.SemaphoreType.DMA((len(pieces_of(rb)), n_chip, 2))
    tp_sem = pltpu.SemaphoreType.DMA((n_tp - 1,))
    like = lambda a: pltpu.VMEM(a.shape, a.dtype)
    return pl.pallas_call(
        functools.partial(kernel, n_ps, n_plane, n_tp, inverse),
        out_shape=jax.ShapeDtypeStruct((EXAMPLES, bank.shape[2]), F32),
        in_specs=[any_spec] * 12,
        out_specs=vmem,
        scratch_shapes=[
            like(x), like(g), like(down), like(up), like(m1a), like(m2a), pltpu.VMEM((rb, 128), F32), pltpu.VMEM((rb, 128), F32), like(bank),
            like(seeds_a), like(seeds_b), pltpu.VMEM((n_plane, rows), jnp.int32),
            pltpu.VMEM((n_plane, rows, pa), BF16),
            pltpu.VMEM((n_plane, rows, pa), BF16),
            pltpu.VMEM((n_plane, pb, 128), BF16),
            pltpu.VMEM((n_plane, pb, 128), BF16),
            pltpu.VMEM((rows, 256), F32),
            pltpu.VMEM((n_tp - 1, rows // n_tp, 256), F32),
            pltpu.VMEM((rows // n_tp, 256), BF16),
            pltpu.VMEM((n_plane, rows, 256), BF16),
            pltpu.VMEM((n_plane * rows, EXAMPLES * 128), BF16),
            pltpu.VMEM((n_plane * rows, EXAMPLES * 128), BF16),
            pltpu.VMEM((n_plane, share, 128), F32),
            pltpu.VMEM((n_plane, share, 128), F32),
            pltpu.VMEM((share, 128), F32),
            pltpu.VMEM((n_tp, share, 128), F32),
            pltpu.VMEM((n_plane, share, 128), F32),
            pltpu.VMEM((EXAMPLES * BANK, 128), F32),
            pltpu.SemaphoreType.DMA((13,)),
            plane_sem, plane_sem, piece_sem, piece_sem, tp_sem, tp_sem, tp_sem, tp_sem, plane_sem, plane_sem,
            plane_sem, plane_sem, tp_sem, tp_sem, plane_sem, plane_sem,
        ],
        compiler_params=pltpu.CompilerParams(
            collective_id=0, has_side_effects=True, vmem_limit_bytes=63 * 1024 * 1024
        ),
    )(x, g, down, up, m1a, m2a, m1b, m2b, seeds_a, seeds_b, segments.reshape(n_plane, rows), bank)


def solution(mesh):
    n_ps, n_tp = mesh.shape["ps"], mesh.shape["tp"]
    n_plane = mesh.shape["ex"] * n_ps
    return jax.shard_map(
        functools.partial(on_device, n_ps, n_plane, n_tp),
        mesh=mesh,
        in_specs=(
            P(("ex", "ps"), "tp"),
            P(("ex", "ps"), "tp"),
            P("tp", None),
            P("tp", None),
            P("tp", ("ex", "ps"), None),
            P("tp", ("ex", "ps"), None),
            P("tp", ("ex", "ps"), None),
            P("tp", ("ex", "ps"), None),
            P("tp", ("ex", "ps")),
            P("tp", ("ex", "ps")),
            P(),
            P(None, None, ("ex", "tp", "ps")),
        ),
        out_specs=P(None, ("ex", "tp", "ps")),
        check_vma=False,
    )
```
